256 devices in a mesh: replica: 16 (over y_lo, z), fsdp: 16 (over y_hi, x, core).
Axes of the slice: x: 4, y: 4 (y_hi: 2, y_lo: 2; y = y_hi * 2 + y_lo), z: 8, core: 2. Of those that a mesh axis runs over, the one named last changes fastest.
Arguments:
- hidden: bfloat16 [16, 4096, 4096], P('replica', 'fsdp'), may hold values from -6 to 6
- key_weight: bfloat16 [16, 4096, 1024], P('replica', 'fsdp'), may hold values from -0.09375 to 0.09375
- adam_first: float32 [16, 4096, 1024], P('replica', 'fsdp'), may hold values from -120 to 120
- adam_second: float32 [16, 4096, 1024], P('replica', 'fsdp'), may hold values from 100 to 4000
- key_cotangent: bfloat16 [16, 4096, 1024], P('replica', 'fsdp'), may hold values from -6 to 6
- frag_global: float32 [4096, 1024], P('fsdp'), may hold values from -6 to 6
- frag_momentum: float32 [4096, 1024], P('fsdp'), may hold values from -3 to 3
- frag_local: bfloat16 [16, 4096, 1024], P('replica', 'fsdp'), may hold values from -6 to 6
Outputs:
- keys: bfloat16 [16, 4096, 1024], P('replica', 'fsdp')
- input_grad: bfloat16 [16, 4096, 4096], P('replica', 'fsdp')
- new_weight: bfloat16 [16, 4096, 1024], P('replica', 'fsdp')
- new_first: float32 [16, 4096, 1024], P('replica', 'fsdp')
- new_second: float32 [16, 4096, 1024], P('replica', 'fsdp')
- new_global: float32 [4096, 1024], P('fsdp')
- new_momentum: float32 [4096, 1024], P('fsdp')
The draws below stay inside these ranges and needn't reach their ends.
All inputs are finite; a program needn't handle non-finite values.
Results may differ from the reference program's by a relative error of at most 0.011.
Values may be sent and summed in bfloat16 or wider, within the bound.
No kernel may reach another device: no remote copies, remote signals or barrier semaphores. Data moves between devices by JAX's collectives and lax.ppermute only.
A program may use at most 128 MiB of HBM per device.

```python
import math
import jax
import jax.numpy as jnp
from jax import lax

D = 4096
KV = 1024
TOKENS = 4096
ISLANDS = 16


def raised(result, stream_key, source, target, shards_of, factor):
    def block_of(dim):
        return (jnp.arange(result.shape[dim]) // (result.shape[dim] // shards_of)).reshape((-1,) + (1,) * (result.ndim - 1 - dim))

    one_side = jax.random.permutation(stream_key, shards_of)[block_of(target)]
    far = (block_of(target) + shards_of // 2) % shards_of
    return jnp.where((block_of(source) == one_side) | (block_of(source) == far), factor * result, result)


def steps_of(key, extent, pieces, low, largest):
    def one(position, parts):
        steps = jax.random.uniform(jax.random.fold_in(jax.random.fold_in(key, 6), position), (parts,), jnp.float32, low / len(pieces), largest / len(pieces))
        return jnp.repeat(jnp.exp(steps), extent[position] // parts).reshape((-1,) + (1,) * (len(extent) - position - 1))

    level = one(*pieces[0])
    for cut in pieces[1:]:
        level = level * one(*cut)
    return level


def noise(key, extent, deviation, limit, split=(), dtype=jnp.bfloat16):
    entries = deviation * jax.random.normal(key, extent, jnp.float32)
    if split:
        entries = entries * steps_of(key, extent, split, -0.22, 0.18)
    return jnp.clip(entries, -limit, limit).astype(dtype)


def noise_with(rng, shape, deviation, limit, split, heavy, held_as=jnp.bfloat16):
    entries = deviation * jax.random.normal(rng, shape, jnp.float32)
    if split:
        entries = entries * steps_of(rng, shape, split, -0.22, 0.18)
    return jnp.clip(raised(entries, jax.random.fold_in(rng, 3), *heavy), -limit, limit).astype(held_as)


def setup_inputs(seed: int = 0) -> dict:
    seeds = jax.random.split(jax.random.key(seed), 9)
    return {
        "hidden": noise_with(seeds[0], (ISLANDS, TOKENS, D), 1.0, 6.0, ((0, 16), (1, 16)), (1, 2, 16, 2.0)),
        "key_weight": noise(seeds[1], (ISLANDS, D, KV), D ** -0.5, 0.09375, ((0, 16), (1, 16))),
        "adam_first": noise(seeds[2], (ISLANDS, D, KV), 20.0, 120.0, ((0, 16), (1, 16)), jnp.float32),
        "adam_second": jnp.clip(jnp.exp(math.log(4000.0) - 3.6888795 * jax.random.uniform(seeds[3], (ISLANDS, D, KV), jnp.float32) ** steps_of(seeds[3], (ISLANDS, D, KV), ((0, 16), (1, 16)), -0.2, 0.2)), 100.0, 4000.0),
        "key_cotangent": noise(seeds[4], (ISLANDS, TOKENS, KV), 1.0, 6.0, ((0, 16), (1, 16))),
        "frag_global": noise(seeds[5], (D, KV), 1.0, 6.0, ((0, 16),), jnp.float32),
        "frag_momentum": noise(seeds[6], (D, KV), 0.5, 3.0, ((0, 16),), jnp.float32),
        "frag_local": noise(seeds[7], (ISLANDS, D, KV), 1.0, 6.0, ((0, 16), (1, 16))),
    }


first_bias = 0.9999734386011124
second_bias = 0.9940794707796655

def island_step(packed):
    inputs, weight, first, second, cotangent = packed
    keys = jnp.dot(inputs, weight, preferred_element_type=jnp.float32).astype(jnp.bfloat16)
    back = lax.dot_general(cotangent, weight, (((1,), (1,)), ((), ())), preferred_element_type=jnp.float32).astype(jnp.bfloat16)
    grad = lax.dot_general(inputs, cotangent, (((0,), (0,)), ((), ())), preferred_element_type=jnp.float32)
    new_first = 0.9 * first + 0.1 * grad
    new_second = 0.95 * second + 0.05 * grad * grad
    update = new_first / first_bias / (jnp.sqrt(new_second / second_bias) + 1e-08)
    old = weight.astype(jnp.float32)
    new_weight = (old - 0.003 * (update + 0.1 * old)).astype(jnp.bfloat16)
    return (keys, back, new_weight, new_first, new_second)

def reference(hidden, key_weight, adam_first, adam_second, key_cotangent, frag_global, frag_momentum, frag_local):
    keys, input_grad, new_weight, new_first, new_second = lax.map(island_step, (hidden, key_weight, adam_first, adam_second, key_cotangent))
    total = lax.optimization_barrier(jnp.sum(frag_global[None, :, :] - frag_local.astype(jnp.float32), axis=0))
    pseudo = total / ISLANDS
    new_momentum = 0.9 * frag_momentum + pseudo
    new_global = frag_global - 0.7 * (pseudo + 0.9 * new_momentum)
    return (keys, input_grad, new_weight, new_first, new_second, new_global, new_momentum)
```

```python
import functools
import jax
import jax.numpy as jnp
import numpy as np
from jax import lax
from jax.experimental import pallas as pl
from jax.experimental.pallas import tpu as pltpu
from jax.sharding import PartitionSpec as P

first_bias = 0.9999734386011124
second_bias = 0.9940794707796655
BF, F32 = jnp.bfloat16, jnp.float32
B = 256
KV = 1024
D = 4096

RELATIVE = ((1, 2), (1, 1), (1, 3), (1, 0), (0, 2), (0, 1), (0, 3), (0, 0))


def places():
    table = np.zeros((256, 24), np.int32)
    for rep in range(16):
        for me in range(16):
            core, x, half = me % 2, me // 2 % 4, me // 8
            row = table[rep * 16 + me]
            for k, (dh, dx) in enumerate(RELATIVE):
                first = (half ^ dh) * 8 + (x + dx) % 4 * 2
                row[k], row[8 + k] = first + core, first + 1 - core
            row[16], row[17], row[18] = rep & 1, rep >> 1 & 1, rep >> 2 & 1
            row[19] = row[16] * 4 + row[17] * 2 + row[18]
    return table


def send(value, dx=0, half=0, core=0):
    pairs = [
        (h * 8 + x * 2 + c, (h ^ half) * 8 + (x + dx) % 4 * 2 + (c ^ core))
        for h in range(2)
        for x in range(4)
        for c in range(2)
    ]
    return lax.ppermute(value, "fsdp", pairs)


def swap(value, bit):
    return lax.ppermute(value, "replica", [(r, r ^ bit) for r in range(16)])


def tdot(a, b):
    return lax.dot_general(a, b, (((0,), (0,)), ((), ())), preferred_element_type=F32)


def ndot(a, b):
    return lax.dot_general(a, b, (((1,), (1,)), ((), ())), preferred_element_type=F32)


def at(shape, row=0, col=0):
    def index(k, s):
        pick = lambda p: p(k, s) if callable(p) else p
        return (pick(row), pick(col))

    return pl.BlockSpec(shape, index)


class Steps:
    def __init__(self, scalars):
        self.scalars = scalars
        self.last = None

    def __call__(self, kernel, ins, outs, grid=1, limit=24, flops=0):
        arrays, specs = [a for a, _ in ins], [s for _, s in ins]
        if self.last is not None:
            arrays.append(self.last)
            specs.append(pl.BlockSpec(memory_space=pl.ANY))
        n, tied = len(ins), self.last is not None

        def run(s, *refs):
            kernel(s, *refs[:n], *refs[n + tied :])

        result = pl.pallas_call(
            run,
            out_shape=[jax.ShapeDtypeStruct(shape, dtype) for shape, dtype, _ in outs],
            grid_spec=pltpu.PrefetchScalarGridSpec(
                num_scalar_prefetch=1,
                grid=(grid,),
                in_specs=specs,
                out_specs=[spec for _, _, spec in outs],
            ),
            compiler_params=pltpu.CompilerParams(vmem_limit_bytes=limit * 2**20),
            cost_estimate=pl.CostEstimate(flops=flops, bytes_accessed=1000, transcendentals=0),
        )(self.scalars, *arrays)
        self.last = result[0]
        return result


def pack_kernel(s, *refs):
    for k in range(8):
        refs[10][:, k * B : (k + 1) * B] = refs[k][...]
    refs[10][:, 2 * KV :] = refs[8][...]
    refs[11][...] = refs[9][...]


def grad_kernel(s, h, ph, c, pc, out):
    out[...] = (tdot(h[...], c[...]) + tdot(ph[...], pc[...])).astype(BF)


def two_kernel(s, h, ph, c, pc, out, last):
    value = (tdot(h[...], c[...]) + tdot(ph[...], pc[...])).astype(BF)

    @pl.when(pl.program_id(0) < 2)
    def _():
        out[...] = value

    @pl.when(pl.program_id(0) == 2)
    def _():
        last[...] = value


def add_kernel(s, h, ph, c, pc, came, out):
    out[...] = (tdot(h[...], c[...]) + tdot(ph[...], pc[...]) + came[...].astype(F32)).astype(BF)


def add_two_kernel(s, h, ph, c, pc, came, one, two):
    value = (tdot(h[...], c[...]) + tdot(ph[...], pc[...]) + came[...].astype(F32)).astype(BF)

    @pl.when(pl.program_id(0) == 0)
    def _():
        one[...] = value

    @pl.when(pl.program_id(0) == 1)
    def _():
        two[...] = value


def adam_kernel(s, h, ph, c, pc, r0, r1, r2, r3, w, m, v, nw, nm, nv):
    grad = tdot(h[...], c[...]) + tdot(ph[...], pc[...])
    grad = grad + r0[...].astype(F32)
    grad = grad + r1[...].astype(F32)
    grad = grad + r2[...].astype(F32)
    grad = grad + r3[...].astype(F32)
    first = 0.9 * m[...] + 0.1 * grad
    second = 0.95 * v[...] + 0.05 * grad * grad
    nm[...] = first
    nv[...] = second
    update = first / first_bias / (jnp.sqrt(second / second_bias) + 1e-08)
    old = w[...].astype(F32)
    nw[...] = (old - 0.003 * (update + 0.1 * old)).astype(BF)


def forward_kernel(s, wh, wl, wr, left, right):
    left[:B] = wh[...]
    left[B:] = wl[...]
    right[:B] = wh[...]
    right[B:] = wr[...]


def copy_two_kernel(s, a, b, left, right):
    left[...] = a[...]
    right[...] = b[...]


def use(hs, phs, c, pc, ws, gi, put):
    a = p = None
    for i, w in enumerate(ws):
        ta = jnp.dot(hs[i][...], w, preferred_element_type=F32)
        tp = jnp.dot(phs[i][...], w, preferred_element_type=F32)
        a, p = (ta, tp) if a is None else (a + ta, p + tp)
        cols = slice(i * B, (i + 1) * B)
        gi[:, cols] = ndot(c[...], w).astype(BF)
        put(cols, ndot(pc[...], w).astype(BF))
    return a, p


def near_kernel(s, *refs):
    hs, phs, (c, pc), ws = refs[:4], refs[4:8], refs[8:10], refs[10:14]
    a, p, gi, pgi = refs[14:]

    def put(cols, value):
        pgi[:, cols] = value

    a[...], p[...] = use(hs, phs, c, pc, [w[...] for w in ws], gi, put)


def far_kernel(s, *refs):
    hs, phs, (c, pc), (l, r, ll, rr) = refs[:4], refs[4:8], refs[8:10], refs[10:14]
    a0, p0, pgi0 = refs[14:17]
    a, gi, out = refs[17:]

    def put(cols, value):
        out[:, slice(KV + cols.start, KV + cols.stop)] = value

    ws = [
        l[:B],
        r[:B],
        jnp.concatenate([l[B:], r[B:]], axis=0),
        jnp.concatenate([ll[...], rr[...]], axis=0),
    ]
    own, peer = use(hs, phs, c, pc, ws, gi, put)
    a[...] = a0[...] + own
    out[:, :KV] = pgi0[...]
    peer = p0[...] + peer
    high = peer.astype(BF)
    out[:, 2 * KV : 3 * KV] = high
    out[:, 3 * KV :] = (peer - high.astype(F32)).astype(BF)


NEAR, FAR = (7, 3, 6, 5), (2, 1, 4, 0)


def finish_kernel(s, a, gi0, gi1, came, keys, out):
    high = came[:, 2 * KV : 3 * KV].astype(F32)
    low = came[:, 3 * KV :].astype(F32)
    keys[...] = (a[...] + (high + low)).astype(BF)
    for j, (order, own) in enumerate(((NEAR, gi0), (FAR, gi1))):
        for i, k in enumerate(order):
            cols = slice(i * B, (i + 1) * B)
            out[:, pl.ds(pl.multiple_of(s[k] * B, B), B)] = own[:, cols]
            other = slice(j * KV + i * B, j * KV + (i + 1) * B)
            out[:, pl.ds(pl.multiple_of(s[8 + k] * B, B), B)] = came[:, other]


def sum1_kernel(s, local, came, keep, give):
    total = local[...].astype(F32) + came[...].astype(F32)
    low, high = total[:64], total[64:]
    mine = s[17] == 0
    keep[...] = jnp.where(mine, low, high)
    give[...] = jnp.where(mine, high, low)


def sum2_kernel(s, held, came, keep, give):
    total = held[...] + came[...]
    low, high = total[:32], total[32:]
    mine = s[18] == 0
    keep[...] = jnp.where(mine, low, high)
    give[...] = jnp.where(mine, high, low)


def sum3_kernel(s, held, came, out):
    out[...] = held[...] + came[...]


def pseudo_kernel(s, held, came, whole, out):
    out[...] = (whole[...] - (held[...] + came[...]) / 16).astype(BF)


def join(first, a, b):
    return jnp.concatenate([jnp.where(first, a, b), jnp.where(first, b, a)], axis=0)


def join_kernel(slot, s, a, b, out):
    out[...] = join(s[slot] == 0, a[...].astype(F32), b[...].astype(F32)).astype(BF)


def merge_kernel(s, a, b, whole, momentum, new_global, new_momentum):
    pseudo = join(s[16] == 0, a[...].astype(F32), b[...].astype(F32))
    after = 0.9 * momentum[...] + pseudo
    new_momentum[...] = after
    new_global[...] = whole[...] - 0.7 * (pseudo + 0.9 * after)


def body(hidden, key_weight, adam_first, adam_second, key_cotangent, frag_global, frag_momentum, frag_local):
    h, w, c = hidden[0], key_weight[0], key_cotangent[0]
    local = frag_local[0]
    device = lax.axis_index("replica") * 16 + lax.axis_index("fsdp")
    step = Steps(lax.dynamic_index_in_dim(jnp.asarray(places()), device, keepdims=False))
    full, square = (B, KV), (B, B)

    def own(k):
        return (h, at(square, 0, lambda _, s, k=k: s[k]))

    def rows(n, row=0):
        return at((n, KV), row)

    w_half = send(w, half=1)
    w_left = send(w, dx=1)
    w_right = send(w, dx=3)

    packed, give = step(
        pack_kernel,
        [(h, at(square, 0, lambda _, s, k=k: s[8 + k])) for k in range(8)]
        + [(c, at(full)), (local, rows(128, lambda _, s: 1 - s[16]))],
        [((B, 3 * KV), BF, at((B, 3 * KV))), ((128, KV), BF, rows(128))],
    )
    peer = send(packed, core=1)
    f1 = swap(give, 1)

    def operands(base):
        return [
            (h, at(square, 0, lambda k, s: s[base + k])),
            (peer, at(square, 0, lambda k, s: base + k)),
            (c, at(full)),
            (peer, at(full, 0, 2)),
        ]

    keep, give = step(
        sum1_kernel,
        [(local, rows(128, lambda _, s: s[16])), (f1, rows(128))],
        [((64, KV), F32, rows(64))] * 2,
    )
    f2 = swap(give, 2)

    (out0,) = step(grad_kernel, operands(0), [(full, BF, at(full))])
    y0 = send(out0, half=1)
    out1, out2 = step(
        two_kernel,
        operands(1),
        [((2 * B, KV), BF, at(full, lambda k, s: jnp.minimum(k, 1))), (full, BF, at(full))],
        grid=3,
    )

    left, right = step(
        forward_kernel,
        [(w_half, at(full)), (w_left, rows(128)), (w_right, rows(128, 1))],
        [((384, KV), BF, rows(384))] * 2,
    )
    s2l = send(left, dx=1)
    s2r = send(right, dx=3)
    y1 = send(out1, half=1)

    acc_a, acc_p, gi0, pgi0 = step(
        near_kernel,
        [own(k) for k in NEAR]
        + [(peer, at(square, 0, k)) for k in NEAR]
        + [(c, at(full)), (peer, at(full, 0, 2))]
        + [(a, at(full)) for a in (w, w_half, w_left, w_right)],
        [(full, F32, at(full))] * 2 + [(full, BF, at(full))] * 2,
    )
    keep, give = step(
        sum2_kernel, [(keep, rows(64)), (f2, rows(64))], [((32, KV), F32, rows(32))] * 2
    )
    f3 = swap(give, 4)

    (sum0,) = step(add_kernel, operands(4) + [(y0, at(full))], [(full, BF, at(full))])
    x2 = send(sum0, dx=2)

    (total,) = step(sum3_kernel, [(keep, rows(32)), (f3, rows(32))], [((32, KV), F32, rows(32))])
    f4 = swap(total, 8)

    left, right = step(
        copy_two_kernel, [(s2l, rows(128)), (s2r, rows(128, 1))], [((128, KV), BF, rows(128))] * 2
    )
    s3l = send(left, dx=1)
    s3r = send(right, dx=3)
    y2 = send(out2, half=1)

    (pseudo,) = step(
        pseudo_kernel,
        [(total, rows(32)), (f4, rows(32)), (frag_global, rows(32, lambda _, s: s[19]))],
        [((32, KV), BF, rows(32))],
    )
    f5 = swap(pseudo, 4)

    acc, gi1, back = step(
        far_kernel,
        [own(k) for k in FAR]
        + [(peer, at(square, 0, k)) for k in FAR]
        + [(c, at(full)), (peer, at(full, 0, 2))]
        + [(s2l, rows(384)), (s2r, rows(384)), (s3l, rows(128)), (s3r, rows(128))]
        + [(a, at(full)) for a in (acc_a, acc_p, pgi0)],
        [(full, F32, at(full)), (full, BF, at(full)), ((B, D), BF, at((B, D)))],
        limit=40,
    )
    got = send(back, core=1)

    (pseudo,) = step(
        functools.partial(join_kernel, 18),
        [(pseudo, rows(32)), (f5, rows(32))],
        [((64, KV), BF, rows(64))],
    )
    f6 = swap(pseudo, 2)

    sum1, sum3 = step(
        add_two_kernel,
        operands(5) + [(y1, at(full, lambda k, s: k))],
        [(full, BF, at(full))] * 2,
        grid=2,
    )
    x1 = send(sum1, dx=1)
    x3 = send(sum3, dx=3)

    (pseudo,) = step(
        functools.partial(join_kernel, 17),
        [(pseudo, rows(64)), (f6, rows(64))],
        [((128, KV), BF, rows(128))],
    )
    f7 = swap(pseudo, 1)

    keys, input_grad = step(
        finish_kernel,
        [(acc, at(full)), (gi0, at(full)), (gi1, at(full)), (got, at((B, D)))],
        [(full, BF, at(full)), ((B, D), BF, at((B, D)))],
    )
    tile = at((B, B), 0, lambda k, s: k)
    new_global, new_momentum = step(
        merge_kernel,
        [(pseudo, at((128, B), 0, lambda k, s: k)), (f7, at((128, B), 0, lambda k, s: k))]
        + [(frag_global, tile), (frag_momentum, tile)],
        [(full, F32, tile)] * 2,
        grid=4,
    )
    new_weight, new_first, new_second = step(
        adam_kernel,
        [own(7), (peer, at(square, 0, 7)), (c, tile), (peer, at(square, 0, lambda k, s: 8 + k))]
        + [(a, tile) for a in (y2, x2, x1, x3, w, adam_first[0], adam_second[0])],
        [(full, BF, tile), (full, F32, tile), (full, F32, tile)],
        grid=4,
    )
    return (
        keys[None],
        input_grad[None],
        new_weight[None],
        new_first[None],
        new_second[None],
        new_global,
        new_momentum,
    )


def solution(mesh):
    rows = P("replica", "fsdp", None)
    return jax.shard_map(
        body,
        mesh=mesh,
        in_specs=(rows,) * 5 + (P("fsdp", None),) * 2 + (rows,),
        out_specs=(rows,) * 5 + (P("fsdp", None),) * 2,
        check_vma=False,
    )
```

```python
import functools
import jax
import jax.numpy as jnp
import numpy as np
from jax import lax
from jax.experimental import pallas as pl
from jax.experimental.pallas import tpu as pltpu
from jax.sharding import PartitionSpec as P

first_bias = 0.9999734386011124
second_bias = 0.9940794707796655
BF, F32 = jnp.bfloat16, jnp.float32
B = 256
KV = 1024
D = 4096
LIMIT = 14 * 2**20
NEAR_COST, USE_COST, FAR_COST = 1_000_000, 1_000_000, 8_000_000

RELATIVE = ((1, 1), (1, 3), (1, 2), (1, 0), (0, 1), (0, 3), (0, 2), (0, 0))


def places():
    table = np.zeros((16, 16), np.int32)
    for me in range(16):
        core, x, half = me % 2, me // 2 % 4, me // 8
        for k, (dh, dx) in enumerate(RELATIVE):
            first = (half ^ dh) * 8 + (x + dx) % 4 * 2
            table[me, k], table[me, 8 + k] = first + core, first + 1 - core
    return table


def send(name, value, dx=0, half=0, core=0):
    pairs = [
        (h * 8 + x * 2 + c, (h ^ half) * 8 + (x + dx) % 4 * 2 + (c ^ core))
        for h in range(2)
        for x in range(4)
        for c in range(2)
    ]
    with jax.named_scope(name):
        return lax.ppermute(value, "fsdp", pairs)


def swap(name, value, flip):
    with jax.named_scope(name):
        return lax.ppermute(value, "replica", [(r, r ^ flip) for r in range(16)])


def tdot(a, b):
    return lax.dot_general(a, b, (((0,), (0,)), ((), ())), preferred_element_type=F32)


def ndot(a, b):
    return lax.dot_general(a, b, (((1,), (1,)), ((), ())), preferred_element_type=F32)


ANY = pl.BlockSpec(memory_space=pl.ANY)


def once(spec, grid):
    if grid > 1 or spec.block_shape is None:
        return spec
    return pl.BlockSpec(spec.block_shape, spec.index_map, pipeline_mode=pl.Buffered(1))


class Steps:
    def __init__(self, scalars):
        self.scalars = scalars
        self.last = None

    def __call__(self, name, kernel, ins, outs, grid=1, cost=1000):
        arrays, specs, n = [a for a, _ in ins], [spec for _, spec in ins], len(ins)
        tied = self.last is not None
        if tied:
            arrays.append(self.last)
            specs.append(ANY)

        def run(s, *refs):
            kernel(s, *refs[:n], *refs[n + tied :])

        result = pl.pallas_call(
            run,
            name=name,
            out_shape=[jax.ShapeDtypeStruct(shape, dtype) for shape, dtype, _ in outs],
            grid_spec=pltpu.PrefetchScalarGridSpec(
                num_scalar_prefetch=1,
                grid=(grid,),
                in_specs=[once(spec, grid) for spec in specs],
                out_specs=[once(spec, grid) for _, _, spec in outs],
            ),
            compiler_params=pltpu.CompilerParams(vmem_limit_bytes=LIMIT),
            cost_estimate=pl.CostEstimate(flops=0, bytes_accessed=cost, transcendentals=0),
        )(self.scalars, *arrays)
        self.last = result[0]
        return result

    def after(self, value):
        return lax.optimization_barrier((value, self.last))[0]


def grad_kernel(s, h, ph, c, pc, *rest):
    out = rest[-1]
    out[...] = (tdot(h[...], c[...]) + tdot(ph[...], pc[...])).astype(BF)


def add_near_kernel(s, h, ph, c, pc, came, _, to_right, to_left):
    value = (tdot(h[...], c[...]) + tdot(ph[...], pc[...]) + came[...].astype(F32)).astype(BF)
    for k, out in enumerate((to_right, to_left)):

        @pl.when(pl.program_id(0) == k)
        def _(out=out):
            out[...] = value


def add_far_kernel(s, h, ph, c, pc, came, right, left, out, own):
    value = tdot(h[...], c[...]) + tdot(ph[...], pc[...]) + came[...].astype(F32)

    @pl.when(pl.program_id(0) == 0)
    def _():
        out[...] = value.astype(BF)

    @pl.when(pl.program_id(0) == 1)
    def _():
        own[...] = value + right[...].astype(F32) + left[...].astype(F32)


def adam_kernel(s, partial, came, w, m, v, nw, nm, nv):
    grad = partial[...] + came[...].astype(F32)
    first = 0.9 * m[...] + 0.1 * grad
    second = 0.95 * v[...] + 0.05 * grad * grad
    nm[...] = first
    nv[...] = second
    scaled = second * (1 / second_bias)
    root = scaled * lax.rsqrt(scaled)
    update = first * (1 / first_bias) / (root + 1e-08)
    old = w[...].astype(F32)
    nw[...] = (old - 0.003 * (update + 0.1 * old)).astype(BF)


def forward_kernel(s, wl, sl, wr, sr, to_right, to_left):
    to_right[:128] = wl[...]
    to_right[128:] = sl[...]
    to_left[:128] = wr[...]
    to_left[128:] = sr[...]


def use(hs, phs, c, pc, ws, gi, pgi):
    a = p = None
    for i, w in enumerate(ws):
        ta = jnp.dot(hs[i][...], w, preferred_element_type=F32)
        tp = jnp.dot(phs[i][...], w, preferred_element_type=F32)
        a, p = (ta, tp) if a is None else (a + ta, p + tp)
        cols = slice(i * B, (i + 1) * B)
        gi[:, cols] = ndot(c[...], w).astype(BF)
        pgi[:, cols] = ndot(pc[...], w).astype(BF)
    return a, p


NEAR, FAR = (7, 3, 5, 4), (1, 0, 6, 2)


def near_kernel(s, *refs):
    hs, phs, (c, pc), ws = refs[:4], refs[4:8], refs[8:10], refs[10:14]
    a, p, gi, pgi = refs[14:]
    a[...], p[...] = use(hs, phs, c, pc, [w[...] for w in ws], gi, pgi)


def far_kernel(s, *refs):
    hs, phs, (c, pc), (l, r, ll, rr) = refs[:4], refs[4:8], refs[8:10], refs[10:14]
    a0, p0, a, gi, pgi, terms = refs[14:]
    ws = [
        l[...],
        r[...],
        jnp.concatenate([ll[:128], rr[:128]], axis=0),
        jnp.concatenate([ll[128:], rr[128:]], axis=0),
    ]
    own, peer = use(hs, phs, c, pc, ws, gi, pgi)
    a[...] = a0[...] + own
    terms[...] = (p0[...] + peer).astype(BF)


def finish_kernel(s, a, gi0, gi1, got0, got1, terms, keys, out):
    keys[...] = (a[...] + terms[...].astype(F32)).astype(BF)
    for order, own, came in ((NEAR, gi0, got0), (FAR, gi1, got1)):
        for i, k in enumerate(order):
            cols = slice(i * B, (i + 1) * B)
            out[:, pl.ds(pl.multiple_of(s[k] * B, B), B)] = own[:, cols]
            out[:, pl.ds(pl.multiple_of(s[8 + k] * B, B), B)] = came[:, cols]


def merge_kernel(s, a, b, whole, momentum, new_global, new_momentum):
    odd = lax.axis_index("replica") % 2
    pseudo = jnp.where(odd == pl.program_id(0), a[...], b[...]) * (1 / 4096)
    after = 0.9 * momentum[...] + pseudo
    new_momentum[...] = after
    new_global[...] = whole[...] - 0.7 * (pseudo + 0.9 * after)


def trade(name, value, flip):
    return swap(name, value.astype(jnp.float16), flip)


def rounded(value):
    return lax.reduce_precision(value, 5, 10)


def body(hidden, key_weight, adam_first, adam_second, key_cotangent, frag_global, frag_momentum, frag_local):
    h, w, c = hidden[0], key_weight[0], key_cotangent[0]
    local = frag_local[0]
    full = (B, KV)

    ph = send("peer_hidden", h, core=1)
    pc = send("peer_cotangent", c, core=1)
    w_half = send("weight_half", w, half=1)
    w_left = send("weight_left", w, dx=1)
    w_right = send("weight_right", w, dx=3)
    f1 = swap("island1", local, 1)

    table = jnp.asarray(places())
    step = Steps(lax.dynamic_index_in_dim(table, lax.axis_index("fsdp"), keepdims=False))
    stay = lambda a: pltpu.with_memory_space_constraint(a, pltpu.HBM)
    h, c = stay(h), stay(c)

    def at(shape, row=0, col=0):
        pick = lambda p, k, s: p(k, s) if callable(p) else p
        return pl.BlockSpec(shape, lambda k, s: (pick(row, k, s), pick(col, k, s)))

    def rows(n, row=0):
        return at((n, KV), row)

    def blocks(base):
        column = at((B, B), 0, lambda k, s: s[base + k])
        return [(h, column), (ph, column), (c, at(full)), (pc, at(full))]

    def chosen(order):
        picks = [at((B, B), 0, lambda _, s, k=k: s[k]) for k in order]
        return [(h, p) for p in picks] + [(ph, p) for p in picks] + [(c, at(full)), (pc, at(full))]

    two = rows(B, lambda k, s: k)
    pair = [(full, BF, at(full))] * 2

    (out,) = step("grad_near", grad_kernel, blocks(0), [((2 * B, KV), BF, two)], grid=2)
    y_near = send("half_near", out, half=1)
    (out,) = step("grad_far", grad_kernel, blocks(2) + [(a, ANY) for a in (w_left, w_right)], [((2 * B, KV), BF, two)], grid=2)
    y_far = send("half_far", out, half=1)
    w_half = step.after(w_half)
    s2l = send("second_left", w_half, dx=1)
    s2r = send("second_right", w_half, dx=3)

    odd = lax.axis_index("replica") % 2
    mine = lambda a: lax.dynamic_slice_in_dim(a, odd * 128, 128)
    difference = (mine(frag_global) * 2 - mine(local).astype(F32) - mine(step.after(f1)).astype(F32)) * 256
    step.last = total = rounded(difference)
    f2 = trade("island2", total, 2)

    acc_a, acc_p, gi0, pgi0 = step(
        "near",
        near_kernel,
        chosen(NEAR) + [(a, at(full)) for a in (w, w_half, w_left, w_right)],
        [(full, F32, at(full))] * 2 + [(full, BF, at(full))] * 2,
    )
    got0 = send("got_near", pgi0, core=1)
    to_right, to_left = step(
        "forward",
        forward_kernel,
        [(w_left, rows(128)), (s2l, rows(128)), (w_right, rows(128, 1)), (s2r, rows(128, 1))],
        pair,
    )
    s3l = send("third_left", to_right, dx=1)
    s3r = send("third_right", to_left, dx=3)

    def summed(name, total, came, flip):
        step.last = total = rounded(total + step.after(came).astype(F32))
        return total, trade(name, total, flip)

    to_right, to_left = step(
        "add_near", add_near_kernel, blocks(4) + [(y_near, two), (got0, ANY)], pair, grid=2, cost=NEAR_COST
    )
    x1 = send("along_right", to_right, dx=1)
    x3 = send("along_left", to_left, dx=3)
    total, f3 = summed("island3", total, f2, 6)
    f3, s3l, s3r = lax.optimization_barrier((f3, s3l, s3r))
    total, f4 = summed("island4", total, f3, 8)

    out, partial = step(
        "add_far",
        add_far_kernel,
        blocks(6) + [(y_far, two), (x1, at(full)), (x3, at(full))],
        [(full, BF, at(full)), (full, F32, at(full))],
        grid=2,
        cost=FAR_COST,
    )
    x2 = send("along_two", out, dx=2)

    acc, gi1, pgi1, terms = step(
        "far",
        far_kernel,
        chosen(FAR) + [(a, at(full)) for a in (s2l, s2r, s3l, s3r, acc_a, acc_p)],
        [(full, F32, at(full))] + [(full, BF, at(full))] * 3,
        cost=USE_COST,
    )
    got1 = send("got_far", pgi1, core=1)
    got2 = send("got_terms", terms, core=1)

    total, f5 = summed("island5", total, f4, 1)

    keys, input_grad = step(
        "finish",
        finish_kernel,
        [(a, at(full)) for a in (acc, gi0, gi1, got0, got1, got2)],
        [(full, BF, at(full)), ((B, D), BF, at((B, D)))],
    )
    tile = rows(64, lambda k, s: k)
    new_weight, new_first, new_second = step(
        "adam",
        adam_kernel,
        [(stay(a), tile) for a in (partial, x2, w, adam_first[0], adam_second[0])],
        [(full, BF, tile), (full, F32, tile), (full, F32, tile)],
        grid=4,
    )
    half = rows(128, lambda k, s: k)
    new_global, new_momentum = step(
        "merge",
        merge_kernel,
        [(total, rows(128)), (step.after(f5).astype(F32), rows(128))]
        + [(stay(a), half) for a in (frag_global, frag_momentum)],
        [(full, F32, half)] * 2,
        grid=2,
    )
    return (
        keys[None],
        input_grad[None],
        new_weight[None],
        new_first[None],
        new_second[None],
        new_global,
        new_momentum,
    )


def solution(mesh):
    rows = P("replica", "fsdp", None)
    return jax.shard_map(
        body,
        mesh=mesh,
        in_specs=(rows,) * 5 + (P("fsdp", None),) * 2 + (rows,),
        out_specs=(rows,) * 5 + (P("fsdp", None),) * 2,
        check_vma=False,
    )
```

```python
import functools
import jax
import jax.numpy as jnp
import numpy as np
from jax import lax
from jax.experimental import pallas as pl
from jax.experimental.pallas import tpu as pltpu
from jax.sharding import PartitionSpec as P

first_bias = 0.9999734386011124
second_bias = 0.9940794707796655
BF, F32 = jnp.bfloat16, jnp.float32
B = 256
KV = 1024
D = 4096
LIMIT = 14 * 2**20

RELATIVE = ((1, 1), (1, 3), (1, 2), (1, 0), (0, 1), (0, 3), (0, 2), (0, 0))


def places():
    table = np.zeros((16, 16), np.int32)
    for me in range(16):
        core, x, half = me % 2, me // 2 % 4, me // 8
        for k, (dh, dx) in enumerate(RELATIVE):
            first = (half ^ dh) * 8 + (x + dx) % 4 * 2
            table[me, k], table[me, 8 + k] = first + core, first + 1 - core
    return table


def send(name, value, dx=0, half=0, core=0):
    pairs = [
        (h * 8 + x * 2 + c, (h ^ half) * 8 + (x + dx) % 4 * 2 + (c ^ core))
        for h in range(2)
        for x in range(4)
        for c in range(2)
    ]
    with jax.named_scope(name):
        return lax.ppermute(value, "fsdp", pairs)


def swap(name, value, flip):
    with jax.named_scope(name):
        return lax.ppermute(value, "replica", [(r, r ^ flip) for r in range(16)])


def tdot(a, b):
    return lax.dot_general(a, b, (((0,), (0,)), ((), ())), preferred_element_type=F32)


def ndot(a, b):
    return lax.dot_general(a, b, (((1,), (1,)), ((), ())), preferred_element_type=F32)


ANY = pl.BlockSpec(memory_space=pl.ANY)


def once(spec, grid):
    if grid > 1 or spec.block_shape is None:
        return spec
    return pl.BlockSpec(spec.block_shape, spec.index_map, pipeline_mode=pl.Buffered(1))


class Steps:
    def __init__(self, scalars):
        self.scalars = scalars
        self.last = None

    def __call__(self, name, kernel, ins, outs, grid=1):
        arrays, specs, n = [a for a, _ in ins], [spec for _, spec in ins], len(ins)
        tied = self.last is not None
        if tied:
            arrays.append(self.last)
            specs.append(ANY)

        def run(s, *refs):
            kernel(s, *refs[:n], *refs[n + tied :])

        result = pl.pallas_call(
            run,
            name=name,
            out_shape=[jax.ShapeDtypeStruct(shape, dtype) for shape, dtype, _ in outs],
            grid_spec=pltpu.PrefetchScalarGridSpec(
                num_scalar_prefetch=1,
                grid=(grid,),
                in_specs=[once(spec, grid) for spec in specs],
                out_specs=[once(spec, grid) for _, _, spec in outs],
            ),
            compiler_params=pltpu.CompilerParams(vmem_limit_bytes=LIMIT),
            cost_estimate=pl.CostEstimate(flops=0, bytes_accessed=1000, transcendentals=0),
        )(self.scalars, *arrays)
        self.last = result[0]
        return result

    def after(self, value):
        return lax.optimization_barrier((value, self.last))[0]


def grad_kernel(s, h, ph, c, pc, out):
    out[...] = (tdot(h[...], c[...]) + tdot(ph[...], pc[...])).astype(BF)


def grad_pair_kernel(s, h, ph, c, pc, *outs):
    value = (tdot(h[...], c[...]) + tdot(ph[...], pc[...])).astype(BF)
    for k, out in enumerate(outs):

        @pl.when(pl.program_id(0) == k)
        def _(out=out):
            out[...] = value


def add_near_kernel(s, h, ph, c, pc, came, _, *outs):
    value = (tdot(h[...], c[...]) + tdot(ph[...], pc[...]) + came[...].astype(F32)).astype(BF)
    for k, out in enumerate(outs):

        @pl.when(pl.program_id(0) == k)
        def _(out=out):
            out[...] = value


def add_two_kernel(s, h, ph, c, pc, came, l, r, out):
    out[...] = (tdot(h[...], c[...]) + tdot(ph[...], pc[...]) + came[...].astype(F32)).astype(BF)


def add_own_kernel(s, h, ph, c, pc, came, right, left, out):
    value = tdot(h[...], c[...]) + tdot(ph[...], pc[...]) + came[...].astype(F32)
    out[...] = value + right[...].astype(F32) + left[...].astype(F32)


def adam_kernel(s, partial, came, w, m, v, nw, nm, nv):
    grad = partial[...] + came[...].astype(F32)
    first = 0.9 * m[...] + 0.1 * grad
    second = 0.95 * v[...] + 0.05 * grad * grad
    nm[...] = first
    nv[...] = second
    scaled = second * (1 / second_bias)
    root = scaled * lax.rsqrt(scaled)
    update = first * (1 / first_bias) / (root + 1e-08)
    old = w[...].astype(F32)
    nw[...] = (old - 0.003 * (update + 0.1 * old)).astype(BF)


def forward_kernel(s, wl, sl, wr, sr, to_right, to_left):
    to_right[:128] = wl[...]
    to_right[128:] = sl[...]
    to_left[:128] = wr[...]
    to_left[128:] = sr[...]


def use(hs, phs, c, pc, ws, gi, pgi):
    a = p = None
    for i, w in enumerate(ws):
        ta = jnp.dot(hs[i][...], w, preferred_element_type=F32)
        tp = jnp.dot(phs[i][...], w, preferred_element_type=F32)
        a, p = (ta, tp) if a is None else (a + ta, p + tp)
        cols = slice(i * B, (i + 1) * B)
        gi[:, cols] = ndot(c[...], w).astype(BF)
        pgi[:, cols] = ndot(pc[...], w).astype(BF)
    return a, p


NEAR, FAR = (7, 3, 5, 4), (1, 0, 6, 2)


def near_kernel(s, *refs):
    hs, phs, (c, pc), ws = refs[:4], refs[4:8], refs[8:10], refs[10:14]
    a, p, gi, pgi = refs[14:]
    a[...], p[...] = use(hs, phs, c, pc, [w[...] for w in ws], gi, pgi)


def far_kernel(s, *refs):
    hs, phs, (c, pc), (l, r, ll, rr) = refs[:4], refs[4:8], refs[8:10], refs[10:14]
    a0, p0, a, gi, pgi, terms = refs[14:]
    ws = [
        l[...],
        r[...],
        jnp.concatenate([ll[:128], rr[:128]], axis=0),
        jnp.concatenate([ll[128:], rr[128:]], axis=0),
    ]
    own, peer = use(hs, phs, c, pc, ws, gi, pgi)
    a[...] = a0[...] + own
    terms[...] = (p0[...] + peer).astype(BF)


def finish_kernel(s, a, gi0, gi1, got0, got1, terms, keys, out):
    keys[...] = (a[...] + terms[...].astype(F32)).astype(BF)
    for order, own, came in ((NEAR, gi0, got0), (FAR, gi1, got1)):
        for i, k in enumerate(order):
            cols = slice(i * B, (i + 1) * B)
            out[:, pl.ds(pl.multiple_of(s[k] * B, B), B)] = own[:, cols]
            out[:, pl.ds(pl.multiple_of(s[8 + k] * B, B), B)] = came[:, cols]


def merge_kernel(s, a, b, whole, momentum, new_global, new_momentum):
    odd = lax.axis_index("replica") % 2
    pseudo = jnp.where(odd == pl.program_id(0), a[...], b[...]) * (1 / 4096)
    after = 0.9 * momentum[...] + pseudo
    new_momentum[...] = after
    new_global[...] = whole[...] - 0.7 * (pseudo + 0.9 * after)


def trade(name, value, flip):
    return swap(name, value.astype(jnp.float16), flip)


def rounded(value):
    return lax.reduce_precision(value, 5, 10)


def body(hidden, key_weight, adam_first, adam_second, key_cotangent, frag_global, frag_momentum, frag_local):
    h, w, c = hidden[0], key_weight[0], key_cotangent[0]
    local = frag_local[0]
    full = (B, KV)

    ph = send("peer_hidden", h, core=1)
    pc = send("peer_cotangent", c, core=1)
    w_half = send("weight_half", w, half=1)
    w_left = send("weight_left", w, dx=1)
    w_right = send("weight_right", w, dx=3)
    f1 = swap("island1", local, 1)

    table = jnp.asarray(places())
    step = Steps(lax.dynamic_index_in_dim(table, lax.axis_index("fsdp"), keepdims=False))
    stay = lambda a: pltpu.with_memory_space_constraint(a, pltpu.HBM)
    h, c = stay(h), stay(c)

    def at(shape, row=0, col=0):
        pick = lambda p, k, s: p(k, s) if callable(p) else p
        return pl.BlockSpec(shape, lambda k, s: (pick(row, k, s), pick(col, k, s)))

    def rows(n, row=0):
        return at((n, KV), row)

    def blocks(base):
        column = at((B, B), 0, lambda k, s: s[base + k])
        return [(h, column), (ph, column), (c, at(full)), (pc, at(full))]

    def chosen(order):
        picks = [at((B, B), 0, lambda _, s, k=k: s[k]) for k in order]
        return [(h, p) for p in picks] + [(ph, p) for p in picks] + [(c, at(full)), (pc, at(full))]

    two = rows(B, lambda k, s: k)
    pair = [(full, BF, at(full))] * 2

    (out,) = step("grad_near", grad_kernel, blocks(0), [((2 * B, KV), BF, two)], grid=2)
    y_near = send("half_near", out, half=1)
    to_two, to_own = step("grad_far", grad_pair_kernel, blocks(2), pair, grid=2)
    y_two = send("half_two", to_two, half=1)
    y_own = send("half_own", to_own, half=1)
    w_half = step.after(w_half)
    s2l = send("second_left", w_half, dx=1)
    s2r = send("second_right", w_half, dx=3)

    odd = lax.axis_index("replica") % 2
    mine = lambda a: lax.dynamic_slice_in_dim(a, odd * 128, 128)
    difference = (mine(frag_global) * 2 - mine(local).astype(F32) - mine(step.after(f1)).astype(F32)) * 256
    step.last = total = rounded(difference)
    f2 = trade("island2", total, 2)

    acc_a, acc_p, gi0, pgi0 = step(
        "near",
        near_kernel,
        chosen(NEAR) + [(a, at(full)) for a in (w, w_half, w_left, w_right)],
        [(full, F32, at(full))] * 2 + [(full, BF, at(full))] * 2,
    )
    got0 = send("got_near", pgi0, core=1)
    to_right, to_left = step(
        "forward",
        forward_kernel,
        [(w_left, rows(128)), (s2l, rows(128)), (w_right, rows(128, 1)), (s2r, rows(128, 1))],
        pair,
    )
    s3l = send("third_left", to_right, dx=1)
    s3r = send("third_right", to_left, dx=3)

    def summed(name, total, came, flip):
        step.last = total = rounded(total + step.after(came).astype(F32))
        return total, trade(name, total, flip)

    to_right, to_left = step(
        "add_near", add_near_kernel, blocks(4) + [(y_near, two), (got0, ANY)], pair, grid=2
    )
    x1 = send("along_right", to_right, dx=1)
    x3 = send("along_left", to_left, dx=3)
    total, f3 = summed("island3", total, f2, 6)

    (out,) = step(
        "add_two",
        add_two_kernel,
        blocks(6) + [(y_two, at(full)), (s3l, ANY), (s3r, ANY)],
        [(full, BF, at(full))],
    )
    x2 = send("along_two", out, dx=2)

    total, f4 = summed("island4", total, f3, 8)

    acc, gi1, pgi1, terms = step(
        "far",
        far_kernel,
        chosen(FAR) + [(a, at(full)) for a in (s2l, s2r, s3l, s3r, acc_a, acc_p)],
        [(full, F32, at(full))] + [(full, BF, at(full))] * 3,
    )
    got1 = send("got_far", pgi1, core=1)
    got2 = send("got_terms", terms, core=1)

    (partial,) = step(
        "add_own",
        add_own_kernel,
        blocks(7) + [(a, at(full)) for a in (y_own, x1, x3)],
        [(full, F32, at(full))],
    )

    total, f5 = summed("island5", total, f4, 1)

    tile = rows(64, lambda k, s: k)
    new_weight, new_first, new_second = step(
        "adam",
        adam_kernel,
        [(partial, tile), (x2, tile)] + [(a, tile) for a in (w, adam_first[0], adam_second[0])],
        [(full, BF, tile), (full, F32, tile), (full, F32, tile)],
        grid=4,
    )
    step.last = stay(step.last)
    keys, input_grad = step(
        "finish",
        finish_kernel,
        [(a, at(full)) for a in (acc, gi0, gi1, got0, got1, got2)],
        [(full, BF, at(full)), ((B, D), BF, at((B, D)))],
    )
    step.last = stay(step.last)
    half = rows(128, lambda k, s: k)
    new_global, new_momentum = step(
        "merge",
        merge_kernel,
        [(total, rows(128)), (step.after(f5).astype(F32), rows(128))]
        + [(a, half) for a in (frag_global, frag_momentum)],
        [(full, F32, half)] * 2,
        grid=2,
    )
    return (
        keys[None],
        input_grad[None],
        new_weight[None],
        new_first[None],
        new_second[None],
        new_global,
        new_momentum,
    )


def solution(mesh):
    rows = P("replica", "fsdp", None)
    return jax.shard_map(
        body,
        mesh=mesh,
        in_specs=(rows,) * 5 + (P("fsdp", None),) * 2 + (rows,),
        out_specs=(rows,) * 5 + (P("fsdp", None),) * 2,
        check_vma=False,
    )
```

```python
import functools
import jax
import jax.numpy as jnp
import numpy as np
from jax import lax
from jax.experimental import pallas as pl
from jax.experimental.pallas import tpu as pltpu
from jax.sharding import PartitionSpec as P

first_bias = 0.9999734386011124
second_bias = 0.9940794707796655
BF, F32 = jnp.bfloat16, jnp.float32
B = 256
KV = 1024
D = 4096
LIMIT = 14 * 2**20

RELATIVE = ((1, 1), (1, 3), (1, 2), (1, 0), (0, 1), (0, 3), (0, 2), (0, 0))


def places():
    table = np.zeros((16, 16), np.int32)
    for me in range(16):
        core, x, half = me % 2, me // 2 % 4, me // 8
        for k, (dh, dx) in enumerate(RELATIVE):
            first = (half ^ dh) * 8 + (x + dx) % 4 * 2
            table[me, k], table[me, 8 + k] = first + core, first + 1 - core
    return table


def send(name, value, dx=0, half=0, core=0):
    pairs = [
        (h * 8 + x * 2 + c, (h ^ half) * 8 + (x + dx) % 4 * 2 + (c ^ core))
        for h in range(2)
        for x in range(4)
        for c in range(2)
    ]
    with jax.named_scope(name):
        return lax.ppermute(value, "fsdp", pairs)


def swap(name, value, flip):
    with jax.named_scope(name):
        return lax.ppermute(value, "replica", [(r, r ^ flip) for r in range(16)])


def tdot(a, b):
    return lax.dot_general(a, b, (((0,), (0,)), ((), ())), preferred_element_type=F32)


def ndot(a, b):
    return lax.dot_general(a, b, (((1,), (1,)), ((), ())), preferred_element_type=F32)


ANY = pl.BlockSpec(memory_space=pl.ANY)


def once(spec, grid):
    if grid > 1 or spec.block_shape is None:
        return spec
    return pl.BlockSpec(spec.block_shape, spec.index_map, pipeline_mode=pl.Buffered(1))


class Steps:
    def __init__(self, scalars):
        self.scalars = scalars
        self.last = None

    def __call__(self, name, kernel, ins, outs, grid=1):
        arrays, specs, n = [a for a, _ in ins], [spec for _, spec in ins], len(ins)
        tied = self.last is not None
        if tied:
            arrays.append(self.last)
            specs.append(ANY)

        def run(s, *refs):
            kernel(s, *refs[:n], *refs[n + tied :])

        result = pl.pallas_call(
            run,
            name=name,
            out_shape=[jax.ShapeDtypeStruct(shape, dtype) for shape, dtype, _ in outs],
            grid_spec=pltpu.PrefetchScalarGridSpec(
                num_scalar_prefetch=1,
                grid=(grid,),
                in_specs=[once(spec, grid) for spec in specs],
                out_specs=[once(spec, grid) for _, _, spec in outs],
            ),
            compiler_params=pltpu.CompilerParams(vmem_limit_bytes=LIMIT),
            cost_estimate=pl.CostEstimate(flops=0, bytes_accessed=1000, transcendentals=0),
        )(self.scalars, *arrays)
        self.last = result[0]
        return result

    def after(self, value):
        return lax.optimization_barrier((value, self.last))[0]


def grad_pair_kernel(s, h, ph, c, pc, *outs):
    value = (tdot(h[...], c[...]) + tdot(ph[...], pc[...])).astype(BF)
    for k, out in enumerate(outs):

        @pl.when(pl.program_id(0) == k)
        def _(out=out):
            out[...] = value


def add_kernel(s, h, ph, c, pc, came, *refs):
    refs[-1][...] = (tdot(h[...], c[...]) + tdot(ph[...], pc[...]) + came[...].astype(F32)).astype(BF)


def add_own_kernel(s, h, ph, c, pc, came, right, left, out):
    value = tdot(h[...], c[...]) + tdot(ph[...], pc[...]) + came[...].astype(F32)
    out[...] = value + right[...].astype(F32) + left[...].astype(F32)


def adam_kernel(s, partial, came, w, m, v, nw, nm, nv):
    grad = partial[...] + came[...].astype(F32)
    first = 0.9 * m[...] + 0.1 * grad
    second = 0.95 * v[...] + 0.05 * grad * grad
    nm[...] = first
    nv[...] = second
    scaled = second * (1 / second_bias)
    root = scaled * lax.rsqrt(scaled)
    update = first * (1 / first_bias) / (root + 1e-08)
    old = w[...].astype(F32)
    nw[...] = (old - 0.003 * (update + 0.1 * old)).astype(BF)


def forward_kernel(s, wl, sl, wr, sr, to_right, to_left):
    to_right[:128] = wl[...]
    to_right[128:] = sl[...]
    to_left[:128] = wr[...]
    to_left[128:] = sr[...]


def use(hs, phs, c, pc, ws, gi, pgi):
    a = p = None
    for i, w in enumerate(ws):
        ta = jnp.dot(hs[i][...], w, preferred_element_type=F32)
        tp = jnp.dot(phs[i][...], w, preferred_element_type=F32)
        a, p = (ta, tp) if a is None else (a + ta, p + tp)
        cols = slice(i * B, (i + 1) * B)
        gi[:, cols] = ndot(c[...], w).astype(BF)
        pgi[:, cols] = ndot(pc[...], w).astype(BF)
    return a, p


NEAR, FAR = (7, 3, 5, 4), (1, 0, 6, 2)


def near_kernel(s, *refs):
    hs, phs, (c, pc), ws = refs[:4], refs[4:8], refs[8:10], refs[10:14]
    a, p, gi, pgi = refs[14:]
    a[...], p[...] = use(hs, phs, c, pc, [w[...] for w in ws], gi, pgi)


def far_kernel(s, *refs):
    hs, phs, (c, pc), (l, r, ll, rr) = refs[:4], refs[4:8], refs[8:10], refs[10:14]
    a0, p0, a, gi, pgi, terms = refs[14:]
    ws = [
        l[...],
        r[...],
        jnp.concatenate([ll[:128], rr[:128]], axis=0),
        jnp.concatenate([ll[128:], rr[128:]], axis=0),
    ]
    own, peer = use(hs, phs, c, pc, ws, gi, pgi)
    a[...] = a0[...] + own
    terms[...] = (p0[...] + peer).astype(BF)


def finish_kernel(s, a, gi0, gi1, got0, got1, terms, keys, out):
    keys[...] = (a[...] + terms[...].astype(F32)).astype(BF)
    for order, own, came in ((NEAR, gi0, got0), (FAR, gi1, got1)):
        for i, k in enumerate(order):
            cols = slice(i * B, (i + 1) * B)
            out[:, pl.ds(pl.multiple_of(s[k] * B, B), B)] = own[:, cols]
            out[:, pl.ds(pl.multiple_of(s[8 + k] * B, B), B)] = came[:, cols]


def merge_kernel(s, a, b, whole, momentum, new_global, new_momentum):
    odd = lax.axis_index("replica") % 2
    pseudo = jnp.where(odd == pl.program_id(0), a[...], b[...]) * (1 / 4096)
    after = 0.9 * momentum[...] + pseudo
    new_momentum[...] = after
    new_global[...] = whole[...] - 0.7 * (pseudo + 0.9 * after)


def trade(name, value, flip):
    return swap(name, value.astype(jnp.float16), flip)


def rounded(value):
    return lax.reduce_precision(value, 5, 10)


def body(hidden, key_weight, adam_first, adam_second, key_cotangent, frag_global, frag_momentum, frag_local):
    h, w, c = hidden[0], key_weight[0], key_cotangent[0]
    local = frag_local[0]
    full = (B, KV)

    ph = send("peer_hidden", h, core=1)
    pc = send("peer_cotangent", c, core=1)
    w_half = send("weight_half", w, half=1)
    w_left = send("weight_left", w, dx=1)
    w_right = send("weight_right", w, dx=3)
    f1 = swap("island1", local, 1)

    table = jnp.asarray(places())
    step = Steps(lax.dynamic_index_in_dim(table, lax.axis_index("fsdp"), keepdims=False))
    stay = lambda a: pltpu.with_memory_space_constraint(a, pltpu.HBM)
    h, c = stay(h), stay(c)

    def at(shape, row=0, col=0):
        pick = lambda p, k, s: p(k, s) if callable(p) else p
        return pl.BlockSpec(shape, lambda k, s: (pick(row, k, s), pick(col, k, s)))

    def rows(n, row=0):
        return at((n, KV), row)

    def blocks(base):
        column = at((B, B), 0, lambda k, s: s[base + k])
        return [(h, column), (ph, column), (c, at(full)), (pc, at(full))]

    def chosen(order):
        picks = [at((B, B), 0, lambda _, s, k=k: s[k]) for k in order]
        return [(h, p) for p in picks] + [(ph, p) for p in picks] + [(c, at(full)), (pc, at(full))]

    pair = [(full, BF, at(full))] * 2

    to_right, to_left = step("grad_near", grad_pair_kernel, blocks(0), pair, grid=2)
    y_right = send("half_right", to_right, half=1)
    y_left = send("half_left", to_left, half=1)
    to_two, to_own = step("grad_far", grad_pair_kernel, blocks(2), pair, grid=2)
    y_two = send("half_two", to_two, half=1)
    y_own = send("half_own", to_own, half=1)
    w_half = step.after(w_half)
    s2l = send("second_left", w_half, dx=1)
    s2r = send("second_right", w_half, dx=3)

    odd = lax.axis_index("replica") % 2
    mine = lambda a: lax.dynamic_slice_in_dim(a, odd * 128, 128)
    difference = (mine(frag_global) * 2 - mine(local).astype(F32) - mine(step.after(f1)).astype(F32)) * 256
    step.last = total = rounded(difference)
    f2 = trade("island2", total, 2)

    acc_a, acc_p, gi0, pgi0 = step(
        "near",
        near_kernel,
        chosen(NEAR) + [(a, at(full)) for a in (w, w_half, w_left, w_right)],
        [(full, F32, at(full))] * 2 + [(full, BF, at(full))] * 2,
    )
    got0 = send("got_near", pgi0, core=1)
    (out,) = step("add_right", add_kernel, blocks(4) + [(y_right, at(full))], [(full, BF, at(full))])
    x1 = send("along_right", out, dx=1)

    to_right, to_left = step(
        "forward",
        forward_kernel,
        [(w_left, rows(128)), (s2l, rows(128)), (w_right, rows(128, 1)), (s2r, rows(128, 1))],
        pair,
    )
    s3l = send("third_left", to_right, dx=1)
    s3r = send("third_right", to_left, dx=3)

    def summed(name, total, came, flip):
        step.last = total = rounded(total + step.after(came).astype(F32))
        return total, trade(name, total, flip)

    (out,) = step("add_left", add_kernel, blocks(5) + [(y_left, at(full)), (got0, ANY)], [(full, BF, at(full))])
    x3 = send("along_left", out, dx=3)

    total, f3 = summed("island3", total, f2, 6)

    (out,) = step(
        "add_two",
        add_kernel,
        blocks(6) + [(y_two, at(full)), (s3l, ANY), (s3r, ANY), (x1, ANY)],
        [(full, BF, at(full))],
    )
    x2 = send("along_two", out, dx=2)

    total, f4 = summed("island4", total, f3, 8)

    acc, gi1, pgi1, terms = step(
        "far",
        far_kernel,
        chosen(FAR) + [(a, at(full)) for a in (s2l, s2r, s3l, s3r, acc_a, acc_p)],
        [(full, F32, at(full))] + [(full, BF, at(full))] * 3,
    )
    got1 = send("got_far", pgi1, core=1)
    got2 = send("got_terms", terms, core=1)

    (partial,) = step(
        "add_own",
        add_own_kernel,
        blocks(7) + [(a, at(full)) for a in (y_own, x1, x3)],
        [(full, F32, at(full))],
    )

    total, f5 = summed("island5", total, f4, 1)

    tile = rows(64, lambda k, s: k)
    new_weight, new_first, new_second = step(
        "adam",
        adam_kernel,
        [(partial, tile), (x2, tile)] + [(a, tile) for a in (w, adam_first[0], adam_second[0])],
        [(full, BF, tile), (full, F32, tile), (full, F32, tile)],
        grid=4,
    )
    step.last = stay(step.last)
    keys, input_grad = step(
        "finish",
        finish_kernel,
        [(a, at(full)) for a in (acc, gi0, gi1, got0, got1, got2)],
        [(full, BF, at(full)), ((B, D), BF, at((B, D)))],
    )
    step.last = stay(step.last)
    half = rows(128, lambda k, s: k)
    new_global, new_momentum = step(
        "merge",
        merge_kernel,
        [(total, rows(128)), (step.after(f5).astype(F32), rows(128))]
        + [(a, half) for a in (frag_global, frag_momentum)],
        [(full, F32, half)] * 2,
        grid=2,
    )
    return (
        keys[None],
        input_grad[None],
        new_weight[None],
        new_first[None],
        new_second[None],
        new_global,
        new_momentum,
    )


def solution(mesh):
    rows = P("replica", "fsdp", None)
    return jax.shard_map(
        body,
        mesh=mesh,
        in_specs=(rows,) * 5 + (P("fsdp", None),) * 2 + (rows,),
        out_specs=(rows,) * 5 + (P("fsdp", None),) * 2,
        check_vma=False,
    )
```
